32 devices in a mesh: row: 4 (over z), col: 8 (over y, x, core).
Axes of the slice: x: 2, y: 2, z: 4, core: 2. Of those that a mesh axis runs over, the one named last changes fastest.
Arguments:
- front_diag: float32 [1024, 1024], replicated, may hold values from -4 to 16, as said below
- panel_rows: float32 [16384, 1024], P(('row', 'col')), may hold values from -1.2 to 1.2
- trailing: float32 [16384, 16384], P('row', 'col'), may hold values from -6 to 6
- pattern: int32 [64, 64], P('row', 'col'), may hold values 0 or 1
Outputs:
- diag_factor: float32 [1024, 1024], replicated
- panel_factor: float32 [16384, 1024], P(('row', 'col'))
- schur: float32 [16384, 16384], P('row', 'col')
The draws below stay inside these ranges and needn't reach their ends.
Inputs may be any that keep to these rules, and one draw needn't show every extreme that they name: front_diag is symmetric and positive definite, with smallest eigenvalue at least 0.5.
All inputs are finite; a program needn't handle non-finite values. No bound on the sum of `pattern` on one device may be relied on, other than what follows from the above.
Results may differ from the reference program's by a relative error of at most 0.0003.
Values sent between devices are 32-bit elements; how exact they have to be, the bound alone decides.
No kernel may reach another device: no remote copies, remote signals or barrier semaphores. Data moves between devices by JAX's collectives and lax.ppermute only.
A program may use at most 192 MiB of HBM per device.

```python
import jax
import jax.numpy as jnp
from jax import lax

W = 512
BLOCK = 256
TRAIL = 16384
PANEL = 1024
NB = 64


def draw_front_diag(key, part):
    order = 2 * W
    first = jax.random.fold_in(key, 11)
    factor = jax.random.normal(first, (order, order), jnp.float32)
    gram = jnp.dot(factor, factor.T, precision=lax.Precision.HIGHEST) / order
    gram = 0.5 * (gram + gram.T)
    ident = jnp.eye(order, dtype=jnp.float32)
    return gram + 0.5 * ident


def set_ends(array, key, low, high):
    longest = array.shape.index(max(array.shape))
    spots = []
    for shift in (0, 1):
        where = [jax.random.randint(jax.random.fold_in(key, axis), (), 0, length) for axis, length in enumerate(array.shape)]
        where[longest] = (where[longest] + shift) % array.shape[longest]
        spots.append(tuple(where))
    return array.at[spots[0]].set(low).at[spots[1]].set(high)


def block_scale(key, extent, pieces, least, top_value):
    gain, own = 1.0, jax.random.fold_in(key, 6)
    for dim, blocks in pieces:
        steps = jnp.exp(jax.random.uniform(jax.random.fold_in(own, dim), (blocks,), jnp.float32, least / len(pieces), top_value / len(pieces)))
        gain = gain * jnp.repeat(steps, extent[dim] // blocks).reshape([-1 if axis == dim else 1 for axis in range(len(extent))])
    return gain


def centred(rng, extent, spread, most, shards=(), kind=jnp.bfloat16):
    level = block_scale(rng, extent, shards, -0.22, 0.18) if shards else 1.0
    result = jax.random.normal(rng, extent, jnp.float32) * spread * level
    return jnp.minimum(jnp.maximum(result, -most), most).astype(kind)


def setup_inputs(seed: int = 0) -> dict:
    streams_of = jax.random.split(jax.random.key(seed), 5)
    front_diag = draw_front_diag(jax.random.fold_in(streams_of[4], 71), 0)
    panel_rows = centred(streams_of[1], (TRAIL, PANEL), 0.2, 1.2, ((0, 32),), jnp.float32)
    trailing = centred(streams_of[2], (TRAIL, TRAIL), 1.0, 6.0, ((0, 4), (1, 8)), jnp.float32)
    pattern = set_ends((jax.random.randint(streams_of[3], (NB, NB), 0, 2) < 1).astype(jnp.int32), jax.random.fold_in(streams_of[3], 1), 0, 1)
    return dict(front_diag=front_diag, panel_rows=panel_rows, trailing=trailing, pattern=pattern)


def reference(front_diag, panel_rows, trailing, pattern):
    diag_factor = jnp.linalg.cholesky(front_diag)
    panel_factor = jax.scipy.linalg.solve_triangular(diag_factor, panel_rows.T, lower=True).T
    blocks = jnp.arange(NB)
    keep = pattern.astype(jnp.float32) * (blocks[:, None] >= blocks[None, :]).astype(jnp.float32)
    column_keep = jnp.repeat(keep, BLOCK, axis=1)

    def one_row(index):
        start = (index * BLOCK).astype(jnp.int32)
        rows = lax.dynamic_slice_in_dim(panel_factor, start, BLOCK, 0)
        update = jnp.dot(rows, panel_factor.T, precision=lax.Precision.HIGHEST)
        old = lax.dynamic_slice_in_dim(trailing, start, BLOCK, 0)
        return old - update * column_keep[index][None, :]
    schur = lax.map(one_row, jnp.arange(NB).astype(jnp.int32)).reshape(TRAIL, TRAIL)
    return (diag_factor, panel_factor, schur)
```

```python
import functools

import jax
import jax.numpy as jnp
import numpy as np
from jax import lax
from jax.experimental import pallas as pl
from jax.experimental.pallas import tpu as pltpu
from jax.sharding import PartitionSpec as P

BLOCK = 256
T = 128
HIGHEST = lax.Precision.HIGHEST
AXES = ("row", "col")
F32, BF16 = jnp.float32, jnp.bfloat16


def tdot(a, b, precision=HIGHEST):
    return lax.dot_general(a, b, (((0,), (0,)), ((), ())), precision=precision, preferred_element_type=F32)


def split2(x):
    hi = x.astype(BF16)
    return hi, (x - hi.astype(F32)).astype(BF16)


def gram8(p):
    h = p.astype(BF16).astype(F32)
    m = (p - h).astype(BF16).astype(F32)
    l = p - h - m
    a = jnp.concatenate([h, h, m, m, h, l], 0).astype(BF16)
    b = jnp.concatenate([h, m, h, m, l, h], 0).astype(BF16)
    return tdot(a, b, None)


def factor_block(d):
    n = len(d)
    lane = lax.broadcasted_iota(jnp.int32, (8, T), 1)
    sub = lax.broadcasted_iota(jnp.int32, (8, T), 0)
    ws, us = [], []
    for g in range(n):
        e = d[g]
        cs = [jnp.broadcast_to(e[:, 8 * g + k : 8 * g + k + 1], (8, T)) for k in range(8)]
        inside = (lane >= 8 * g) & (lane < 8 * g + 8)
        e = jnp.where(inside, jnp.where(lane - 8 * g == sub, 1.0, 0.0), e)
        piv = jnp.ones((8, T), F32)
        for j in range(8):
            p = jnp.broadcast_to(cs[j][j : j + 1], (8, T))
            piv = jnp.where(sub == j, p, piv)
            if j == 7:
                break
            m = jnp.where(sub > j, cs[j] * (1.0 / p), 0.0)
            for k in range(j + 1, 8):
                cs[k] = cs[k] - m * jnp.broadcast_to(cs[k][j : j + 1], (8, T))
            e = e - m * jnp.broadcast_to(e[j : j + 1], (8, T))
        r = lax.rsqrt(piv)
        r = r * (1.5 - 0.5 * piv * r * r)
        e = e * r
        u = jnp.zeros((8, T), F32)
        for k in range(8):
            u = jnp.where((lane == 8 * g + k) & (sub <= k), cs[k] * r, u)
        us.append(jnp.where(lane >= 8 * g + 8, e, u))
        ws.append(jnp.where(lane < 8 * g + 8, e, 0.0))
        if g + 1 < n:
            update = gram8(e)
            for i in range(g + 1, n):
                d[i] = jnp.where(inside, 0.0, d[i]) - update[8 * i : 8 * i + 8]
    return ws, us


def factor_kernel(a_ref, old_ref, l_ref, inv_ref, new_ref, s_ref, w_ref, u_ref, p_ref, stage, sem):
    n = a_ref.shape[0]
    nb = n // T
    share = old_ref.shape[0] // nb

    def load(b):
        rows = pl.ds(pl.multiple_of(b * share, share), share)
        return pltpu.make_async_copy(old_ref.at[rows], stage.at[lax.rem(b, 2)], sem.at[lax.rem(b, 2)])

    def store(b):
        rows = pl.ds(pl.multiple_of(b * share, share), share)
        return pltpu.make_async_copy(stage.at[lax.rem(b, 2)], new_ref.at[rows], sem.at[2 + lax.rem(b, 2)])

    load(0).start()
    s_ref[...] = a_ref[...]
    l_ref[...] = jnp.zeros_like(l_ref)
    inv_ref[...] = jnp.zeros_like(inv_ref)
    colb = lax.broadcasted_iota(jnp.int32, (T, n), 1) // T

    @pl.loop(0, nb)
    def _(b):
        load(b).wait()
        store(b).start()

        @pl.when(b + 1 < nb)
        def _():
            @pl.when(b >= 1)
            def _():
                store(b - 1).wait()

            load(b + 1).start()

        here = pl.ds(pl.multiple_of(b * T, T), T)
        block = s_ref[here, here]
        ws, us = factor_block([block[8 * g : 8 * g + 8] for g in range(T // 8)])
        for g in range(T // 8):
            w_ref[8 * g : 8 * g + 8, :] = ws[g]
            u_ref[8 * g : 8 * g + 8, :] = us[g]
        w = w_ref[...]
        p_ref[...] = jnp.dot(w, s_ref[here, :], precision=HIGHEST, preferred_element_type=F32)
        p_ref[:, here] = w
        inv_ref[here, :] = jnp.where(colb <= b, p_ref[...], 0.0)
        l_ref[here, here] = u_ref[...].T

        @pl.loop(b + 1, nb)
        def _(i):
            there = pl.ds(pl.multiple_of(i * T, T), T)
            ui = p_ref[:, there]
            s_ref[there, :] = jnp.where(colb == b, 0.0, s_ref[there, :]) - tdot(ui, p_ref[...])
            l_ref[there, here] = ui.T

    if nb > 1:
        store(nb - 2).wait()
    store(nb - 1).wait()


VMEM = pl.BlockSpec(memory_space=pltpu.VMEM)
ANY = pl.BlockSpec(memory_space=pl.ANY)
BIG = pltpu.CompilerParams(vmem_limit_bytes=58 << 20)


def cost(flops, moved):
    return pl.CostEstimate(flops=int(flops), bytes_accessed=int(moved), transcendentals=0)


def factor(a, old):
    n = a.shape[0]
    full = jax.ShapeDtypeStruct((n, n), F32)
    return pl.pallas_call(
        factor_kernel,
        out_shape=(full, full, jax.ShapeDtypeStruct(old.shape, F32)),
        in_specs=[VMEM, ANY],
        out_specs=(VMEM, VMEM, ANY),
        scratch_shapes=[
            pltpu.VMEM((n, n), F32),
            pltpu.VMEM((T, T), F32),
            pltpu.VMEM((T, T), F32),
            pltpu.VMEM((T, n), F32),
            pltpu.VMEM((2, old.shape[0] * T // n, old.shape[1]), F32),
            pltpu.SemaphoreType.DMA((4,)),
        ],
        compiler_params=BIG,
        cost_estimate=cost(8e10, 12 << 20),
        name="factor",
    )(a, old)


def dot3(a_hi, a_lo, b_hi, b_lo):
    dot = functools.partial(jnp.dot, preferred_element_type=F32)
    return dot(a_hi, b_hi) + dot(a_lo, b_hi) + dot(a_hi, b_lo)


def inverse_kernel(inv_ref, rows_ref, x_ref, cat_ref, lt_hi, lt_lo, in_hi, in_lo, r_hi, r_lo):
    n = inv_ref.shape[0]

    @pl.loop(0, n // T)
    def _(k):
        part = pl.ds(pl.multiple_of(k * T, T), T)
        v = inv_ref[part, :]
        in_hi[part, :], in_lo[part, :] = split2(v)
        lt_hi[:, part], lt_lo[:, part] = split2(v.T)

    r_hi[...], r_lo[...] = split2(rows_ref[...])
    step = min(n, 256)
    for j in range(n // step):
        cols, deep = slice(j * step, (j + 1) * step), slice(0, (j + 1) * step)
        x_ref[:, cols] = dot3(r_hi[:, deep], r_lo[:, deep], lt_hi[deep, cols], lt_lo[deep, cols])
    for i in range(n // step):
        rows, deep = slice(i * step, (i + 1) * step), slice(i * step, n)
        cat_ref[rows, :], cat_ref[n + i * step : n + (i + 1) * step, :] = split2(dot3(lt_hi[rows, deep], lt_lo[rows, deep], in_hi[deep, :], in_lo[deep, :]))


def inverse(inv, rows):
    n, m = inv.shape[0], rows.shape[0]
    return pl.pallas_call(
        inverse_kernel,
        out_shape=(jax.ShapeDtypeStruct((m, n), F32), jax.ShapeDtypeStruct((2 * n, n), BF16)),
        in_specs=[VMEM] * 2,
        out_specs=(VMEM,) * 2,
        scratch_shapes=[pltpu.VMEM((n, n), BF16)] * 4 + [pltpu.VMEM((m, n), BF16)] * 2,
        compiler_params=BIG,
        cost_estimate=cost(8 * n * n * n, 16 << 20),
        name="inverse",
    )(inv, rows)


def pick_kernel(layout, info, *refs):
    arrays, outs, (buf, in_sem, out_sem) = refs[: layout["arrays"]], refs[layout["arrays"] : -3], refs[-3:]
    moves, at = [], 0
    for out, segments in zip(outs, layout["segments"]):
        for to, size, choices, entry in segments:
            moves.append((out, to, size, choices, entry, at))
            at += size
    for wait in (False, True):
        for number, (out, to, size, choices, entry, at) in enumerate(moves):
            stage = buf.at[pl.ds(at, size)]
            store = pltpu.make_async_copy(stage, out.at[pl.ds(to, size)], out_sem.at[number])
            for n, (frm, off) in enumerate(choices):
                load = pltpu.make_async_copy(arrays[frm].at[pl.ds(off, size)], stage, in_sem.at[number])

                @pl.when(True if entry is None else info[entry] == n)
                def _(load=load, store=store):
                    if wait:
                        load.wait()
                        store.start()
                    else:
                        load.start()
    for number, (out, to, size, choices, entry, at) in enumerate(moves):
        store = pltpu.make_async_copy(buf.at[pl.ds(at, size)], out.at[pl.ds(to, size)], out_sem.at[number])

        @pl.when(True if entry is None else info[entry] >= 0)
        def _(store=store):
            store.wait()


def pick(info, arrays, segments):
    cols = arrays[0].shape[1]
    count = sum(map(len, segments))
    return pl.pallas_call(
        functools.partial(pick_kernel, dict(arrays=len(arrays), segments=segments)),
        out_shape=tuple(jax.ShapeDtypeStruct((sum(s[1] for s in seg), cols), F32) for seg in segments),
        grid_spec=pltpu.PrefetchScalarGridSpec(
            num_scalar_prefetch=1,
            grid=(1,),
            in_specs=[ANY] * len(arrays),
            out_specs=(ANY,) * len(segments),
            scratch_shapes=[
                pltpu.VMEM((sum(s[1] for seg in segments for s in seg), cols), F32),
                pltpu.SemaphoreType.DMA((count,)),
                pltpu.SemaphoreType.DMA((count,)),
            ],
        ),
        compiler_params=BIG,
        cost_estimate=cost(1000, 1000),
        name="pick",
    )(info, *arrays)


AHEAD, RING, SLOTS, GROUP = 4, 12, 4, 4


def update_kernel(layout, info, pattern, *refs):
    pieces, parts, tiles = (layout[k] for k in ("pieces", "parts", "tiles"))
    tile, sub, part = (layout[k] for k in ("tile", "sub", "part"))
    keeps_rows, gives, near = layout["keeps_rows"], layout["gives"], layout["near"]
    refs = list(refs)
    take = lambda k: [refs.pop(0) for _ in range(k)]
    sources = [take(p["sources"]) for p in pieces]
    ready = [take(1)[0] if p["ready"] is not None else None for p in pieces]
    part_refs, cat_ref = take(len(parts)), take(1)[0]
    take(1 + layout["rows_in"])
    out, rows_hbm, given = take(1)[0], (take(layout["rows_any"]) or [None])[0], (take(1 if gives else 0) or [None])[0]
    cat, p_buf, ht, row_f32, rows_v, block, flat, sem, p_sem, ht_sem, f32_sem, row_sem, in_sem, out_sem = refs
    count, steps = len(pieces), len(tiles)
    buffer = [sum(p["fresh"] for p in pieces[:m]) for m in range(count)]
    width, n = p_buf.shape[1:]
    subs = width // sub
    each = count * subs
    rb, cb = out.shape[0] // BLOCK, out.shape[1] // BLOCK
    r, c, diag = info[0], info[1], info[3] == 1

    def row_of(step):
        at = step * tile
        return (jnp.bitwise_xor(at // part, c) * part) + at % part

    def col_of(m, s):
        q = info[pieces[0]["number"]]
        for k in range(1, count):
            q = jnp.where(m == k, info[pieces[k]["number"]], q)
        return q * width + s * sub

    def place(t):
        e = flat[t]
        return e // each, (e % each) // subs, e % subs

    def view(t):
        step, m, s = place(t)
        row, col = pl.multiple_of(row_of(step), tile), pl.multiple_of(col_of(m, s), sub)
        return out.at[pl.ds(row, tile), pl.ds(col, sub)]

    def load(t):
        return pltpu.make_async_copy(view(t), block.at[lax.rem(t, RING)], in_sem.at[lax.rem(t, RING)])

    def store(t):
        return pltpu.make_async_copy(block.at[lax.rem(t, RING)], view(t), out_sem.at[lax.rem(t, RING)])

    def prefetch(t, total):
        @pl.when(t < total)
        def _():
            @pl.when(t >= RING)
            def _():
                store(t - RING).wait()

            load(t).start()

    def every(copies, what):
        for yes, copy in copies:
            if yes is True:
                getattr(copy, what)()
            else:
                @pl.when(yes)
                def _(copy=copy):
                    getattr(copy, what)()

    @pl.when(info[layout["needed"]] == 1)
    def _():
        copy = pltpu.make_async_copy
        cats = [(True, copy(cat_ref, cat, sem.at[0]))]
        loads = [[] for _ in pieces]
        for m, p in enumerate(pieces):
            for k in range(p["sources"]):
                chosen = (info[p["where"]] == k) if p["sources"] > 1 else True
                loads[m].append((jnp.logical_not(diag) & chosen, copy(sources[m][k], p_buf.at[buffer[m]], p_sem.at[m, k])))
            if p["fresh"]:
                for k, (mask, off, size, frm) in enumerate(parts):
                    to = p_buf.at[buffer[m], pl.ds(off, size)]
                    loads[m].append((diag & (info[p["mask"]] == mask), copy(part_refs[k].at[pl.ds(frm, size)], to, p_sem.at[m, 2 + k])))
        hts = []
        for m, p in enumerate(pieces):
            if p["ready"] is not None:
                src = ready[m].at[pl.ds(p["ready"] * width, width)]
                yes = jnp.logical_not(diag) if p["fresh"] else True
                hts.append((yes, copy(src, ht.at[m], ht_sem.at[m])))
        stored = [t for t, (k, _) in enumerate(tiles) if k is None]
        floats = [t for t, (k, _) in enumerate(tiles) if k is not None]
        rows = [(True, copy(rows_hbm.at[pl.ds(t * tile, tile)], rows_v.at[pl.ds(t * tile, tile)], row_sem.at[t])) for t in stored]

        def float_copy(u):
            k, off = tiles[floats[u]]
            return copy(part_refs[k].at[pl.ds(off, tile)], row_f32.at[u % SLOTS], f32_sem.at[u % SLOTS])

        def keep_copy(u):
            here = pl.ds(floats[u] * tile, tile)
            return copy(rows_v.at[here], rows_hbm.at[here], row_sem.at[floats[u]])

        for m in range(count):
            every(loads[m], "start")
        every(cats, "start")

        def note(e, found):
            step, m, s = e // each, (e % each) // subs, e % subs
            row, col = row_of(step) // BLOCK, col_of(m, s) // BLOCK
            flat[found] = e
            kept = (pattern[row, col] == 1) & (r * rb + row >= c * cb + col)
            if near:
                now = step >= near
                for k, p in enumerate(pieces):
                    now = now | ((m == k) & (diag if p["ready"] is not None else True)) if p["fresh"] else now
                kept = kept & now
            return found + kept.astype(jnp.int32)

        total = lax.fori_loop(0, steps * each, note, 0)
        for t in range(AHEAD):
            prefetch(t, total)

        step = min(width, 256)
        chunks = [(m, at) for m, p in enumerate(pieces) if p["fresh"] for at in range(0, width, step)]
        gone = []
        for number, (m, at) in enumerate(chunks):
            if at == 0:
                every(loads[m], "wait")
            if number == 0:
                every(cats, "wait")
                for u in range(min(SLOTS, len(floats))):
                    float_copy(u).start()
                every(rows, "start")
                every(hts, "start")
            here = slice(at, at + step)

            def multiply(m=m, here=here):
                hi, lo = split2(p_buf[buffer[m], here])
                ht[m, here, :n], ht[m, here, n:] = split2(dot3(hi, lo, cat[:n], cat[n:]))

            if pieces[m]["ready"] is None:
                multiply()
            else:
                pl.when(diag)(multiply)
            if gives and at + step == width:
                gone.append((True, copy(ht.at[m], given.at[pl.ds(m * width, width)], sem.at[1 + m])))
                every(gone[-1:], "start")
            share = [u for u in range(len(floats)) if u * len(chunks) // len(floats) == number]
            for u in share:
                float_copy(u).wait()
                rows_at = pl.ds(floats[u] * tile, tile)
                rows_v[rows_at, :n], rows_v[rows_at, n:] = split2(row_f32[u % SLOTS])
                if u + SLOTS < len(floats):
                    float_copy(u + SLOTS).start()
                if keeps_rows:
                    keep_copy(u).start()
        every(hts, "wait")
        every(rows, "wait")

        def product(t):
            tile_at, m, s = place(t)
            mine = rows_v[pl.ds(pl.multiple_of(tile_at * tile, tile), tile), :]
            cols = pl.ds(pl.multiple_of(s * sub, sub), sub)
            dot = functools.partial(lax.dot_general, dimension_numbers=(((1,), (1,)), ((), ())), preferred_element_type=F32)
            return dot(mine[:, :n], ht[m, cols, :n]) + dot(mine[:, n:], ht[m, cols, :n]) + dot(mine[:, :n], ht[m, cols, n:])

        def finish(t, value):
            load(t).wait()
            block[lax.rem(t, RING)] = block[lax.rem(t, RING)] - value
            store(t).start()

        def work(t, size):
            for k in range(size):
                prefetch(t + k + AHEAD, total)
            values = [product(t + k) for k in range(size)]
            for k in range(size):
                finish(t + k, values[k])

        whole = total // GROUP * GROUP

        @pl.loop(0, whole, step=GROUP)
        def _(t):
            work(t, GROUP)

        @pl.loop(whole, total)
        def _(t):
            work(t, 1)

        @pl.loop(jnp.maximum(total - RING, 0), total)
        def _(t):
            store(t).wait()

        every(gone, "wait")
        if keeps_rows:
            for u in range(len(floats)):
                keep_copy(u).wait()


def update(info, pattern, pieces, parts, tiles, near, needed, tile, part, cat, schur, rows, keeps_rows, gives):
    n = cat.shape[1]
    width = next(p[3][0].shape[0] for p in pieces if p[3])
    local_rows, local_cols = schur.shape
    sub = min(width, BLOCK)
    count, steps = len(pieces), len(tiles)
    layout = dict(
        pieces=[
            dict(number=a, mask=b, where=w, sources=len(x), ready=None if y is None else y[1], fresh=b is not None)
            for a, b, w, x, y in pieces
        ],
        parts=[(mask, off, size, frm) for mask, off, size, _, frm in parts],
        tiles=tiles,
        near=near,
        needed=needed,
        tile=tile,
        sub=sub,
        part=part,
        keeps_rows=keeps_rows,
        gives=gives,
        rows_in=0 if rows is None else 1,
        rows_any=1 if keeps_rows or rows is not None else 0,
    )
    operands = [x for p in pieces for x in p[3]] + [p[4][0] for p in pieces if p[4] is not None] + [p[3] for p in parts] + [cat, schur]
    aliases = {2 + len(operands) - 1: 0}
    shapes = [jax.ShapeDtypeStruct(schur.shape, F32)]
    if rows is not None:
        operands.append(rows)
        aliases[2 + len(operands) - 1] = 1
    if layout["rows_any"]:
        shapes.append(jax.ShapeDtypeStruct((local_rows, 2 * n), BF16))
    if gives:
        shapes.append(jax.ShapeDtypeStruct((count * width, 2 * n), BF16))
    dma = pltpu.SemaphoreType.DMA
    return pl.pallas_call(
        functools.partial(update_kernel, layout),
        out_shape=tuple(shapes),
        grid_spec=pltpu.PrefetchScalarGridSpec(
            num_scalar_prefetch=2,
            grid=(1,),
            in_specs=[ANY] * len(operands),
            out_specs=(ANY,) * len(shapes),
            scratch_shapes=[
                pltpu.VMEM((2 * n, n), BF16),
                pltpu.VMEM((sum(p["fresh"] for p in layout["pieces"]), width, n), F32),
                pltpu.VMEM((count, width, 2 * n), BF16),
                pltpu.VMEM((SLOTS, tile, n), F32),
                pltpu.VMEM((steps * tile, 2 * n), BF16),
                pltpu.VMEM((RING, tile, sub), F32),
                pltpu.SMEM((steps * count * (width // sub) + 1,), jnp.int32),
                dma((2 + count,)),
                dma((count, 2 + len(parts))),
                dma((count,)),
                dma((SLOTS,)),
                dma((steps,)),
                dma((RING,)),
                dma((RING,)),
            ],
        ),
        input_output_aliases=aliases,
        compiler_params=BIG,
        cost_estimate=cost(1000, 1000),
        name="update",
    )(info, pattern, *operands)


def plan(nrow, ncol):
    half, ratio = nrow // 2, ncol // nrow
    if (nrow, ncol) != (4, 8):
        shift = {nrow - 1: 0, nrow - 2: half}
        free = [g for g in range(1, nrow) if g != half]
        for i in range(nrow - 2):
            shift[i] = free[i]
        rounds = [{} for _ in range(nrow)]
        for m in range(nrow):
            for i in range(nrow):
                for j in range(i * ratio):
                    q = m ^ shift[i]
                    rounds[m][i, j] = (divmod(j * nrow + q, ncol), "own", q)
        return rounds
    rounds = [{} for _ in range(4)]

    def at(z, y, x, k):
        return z, (y * 2 + x) * 2 + k

    def put(m, to, frm, kind, x, k):
        rounds[m][at(*to)] = (at(*frm), kind, 2 * x + k)

    first = {0: (0, 1), 1: (0, 0), 2: (1, 0)}
    for z in (1, 2, 3):
        for src in range(z):
            y, x = divmod(src, 2)
            for core in (0, 1):
                half_x = first[src][core] if z != 2 else 1 - first[src][core]
                for m in (0, 1):
                    k = m if z != 1 else 1 - m
                    put(m, (z, y, x, core), (src, core, half_x, k), "own", half_x, k)
    put(2, (3, 0, 0, 0), (0, 0, 0, 0), "x", 1, 0)
    put(2, (3, 0, 0, 1), (0, 0, 0, 1), "y", 0, 1)
    put(3, (3, 0, 0, 0), (0, 0, 0, 1), "x", 1, 1)
    put(3, (3, 0, 0, 1), (0, 1, 1, 0), "x", 0, 0)
    put(2, (3, 0, 1, 0), (1, 0, 1, 0), "own", 1, 0)
    put(2, (3, 0, 1, 1), (1, 0, 1, 1), "y", 1, 1)
    put(3, (3, 0, 1, 0), (1, 0, 1, 1), "own", 1, 1)
    put(3, (3, 0, 1, 1), (1, 1, 1, 0), "own", 1, 0)
    put(2, (3, 1, 0, 1), (2, 1, 0, 0), "x", 1, 0)
    put(2, (3, 1, 0, 0), (2, 1, 0, 1), "y", 0, 1)
    put(3, (3, 1, 0, 1), (2, 1, 1, 1), "own", 1, 1)
    put(3, (3, 1, 0, 0), (2, 1, 0, 0), "y", 0, 0)
    put(2, (2, 0, 0, 0), (3, 0, 0, 0), "a", 0, 0)
    put(3, (2, 0, 0, 0), (3, 0, 0, 0), "b", 0, 1)
    put(2, (2, 0, 0, 1), (3, 0, 0, 1), "a", 1, 0)
    put(3, (2, 0, 0, 1), (0, 1, 1, 1), "own", 1, 1)
    put(2, (2, 0, 1, 0), (3, 0, 1, 0), "a", 0, 0)
    put(3, (2, 0, 1, 0), (3, 0, 1, 0), "b", 0, 1)
    put(2, (2, 0, 1, 1), (3, 0, 1, 1), "a", 0, 0)
    put(3, (2, 0, 1, 1), (1, 1, 0, 1), "own", 0, 1)
    for m in (2, 3):
        put(m, (1, 0, 0, 0), (0, 0, 1, m - 2), "own", 1, m - 2)
        put(m, (1, 0, 0, 1), (0, 1, 0, m - 2), "own", 0, m - 2)
    return rounds


KINDS = ("own", "x", "y", "a", "b")


def tables(nrow, ncol, rounds):
    ratio = ncol // nrow
    tight = (nrow, ncol) == (4, 8)
    out = []
    for i in range(nrow):
        for j in range(ncol):
            qs = []
            for m in range(nrow):
                if (i, j) in rounds[m]:
                    qs.append(rounds[m][i, j][2])
                elif tight:
                    qs.append(m ^ (2 * ((j >> 1) & 1)))
                else:
                    qs.append(m)
            masks = [((j * nrow + q) % ncol) ^ j for q in qs]
            sent = [-1] * nrow
            for m in range(nrow):
                for (frm, kind, _) in rounds[m].values():
                    if frm == (i, j):
                        sent[m] = KINDS.index(kind)
            late = int(tight and is_late((i, j)))
            out.append([i, j, int(i >= j // ratio), int(i == j // ratio), *qs, *masks, *sent, late, int(i > j // ratio)])
    return np.array(out, np.int32)


def is_late(to):
    return to in ((3, 0), (3, 2), (3, 4))


def local(nrow, ncol, front_diag, panel_rows, trailing, pattern):
    local_rows = trailing.shape[0]
    part = panel_rows.shape[0]
    half = nrow // 2
    everyone = [(i, j) for i in range(nrow) for j in range(ncol)]
    rounds = plan(nrow, ncol)
    info = jnp.asarray(tables(nrow, ncol, rounds))[lax.axis_index("row") * ncol + lax.axis_index("col")]
    piece_at, mask_at, sent_at, late_at = 4, 4 + nrow, 4 + 2 * nrow, 4 + 3 * nrow
    barrier = lax.optimization_barrier

    def across(x, mask):
        return lax.ppermute(x, AXES, [(i * ncol + j, i * ncol + (j ^ mask)) for i, j in everyone])

    def send(x, moves):
        return lax.ppermute(x, AXES, [(a * ncol + b, i * ncol + j) for (i, j), ((a, b), _, _) in moves.items()])

    tight = (nrow, ncol) == (4, 8)
    tile = min(BLOCK, part // 2 if tight else part)
    per = part // tile
    below_at = late_at + 1

    def fresh(m, *sources, ready=None):
        return piece_at + m, mask_at + m, late_at, sources, ready

    def cut(parts):
        return [(k, frm + s) for k, (_, _, size, _, frm) in enumerate(parts) for s in range(0, size, tile)]

    def stored(steps):
        return [(None, t * tile) for t in range(steps)]

    def change(pieces, parts, tiles, s, rows, near=0, needed=2, keeps=False, gives=False):
        return update(info, pattern, pieces, parts, tiles, near, needed, tile, part, cat, s, rows, keeps, gives)

    near = [m for m in range(2, ncol, 2) if not (tight and m == 6)]
    got = {m: across(panel_rows, m) for m in near}
    col = [send(panel_rows, rounds[m]) for m in range(half)]
    other = across(panel_rows, 1)
    diag_factor, inv, schur = factor(front_diag, trailing)
    panel_factor, cat = inverse(inv, panel_rows)
    held, cat = barrier(([panel_rows, other, *[got[m] for m in near], *col], cat))
    own, other, got, col = held[0], held[1], dict(zip(near, held[2:])), held[2 + len(near) :]

    if not tight:
        parts = [(0, 0, part, own, 0), (1, 0, part, other, 0)]
        for m in near:
            parts += [(m, 0, part, got[m], 0), (m + 1, 0, part, across(got[m], 1), 0)]
        col = [*col, *[send(own, rounds[m]) for m in range(half, nrow)]]
        parts.sort(key=lambda p: p[0])
        one, two = [[fresh(m, col[m]) for m in ms] for ms in (range(half), range(half, nrow))]
        schur, rows = change(one, parts, cut(parts), schur, None, keeps=True)
        schur, _ = change(two, parts, stored(ncol * per), schur, rows)
        return (diag_factor, panel_factor, schur)

    h = part // 2
    arrays = [own, got[2], got[4], col[0], col[1]]
    choices = [(k, 0) for k in range(5)]
    c_op, d_op, h1, h2 = pick(
        info,
        arrays,
        [
            [(0, part, choices, sent_at + 2)],
            [(0, part, choices, sent_at + 3)],
            [(0, h, [(1, 0)], None)],
            [(0, h, [(2, h)], None)],
        ],
    )
    c = send(c_op, rounds[2])
    d_early = send(d_op, {to: move for to, move in rounds[3].items() if not is_late(to)})
    got[3], got[5] = across(got[2], 1), across(got[4], 1)
    h1, h2 = across(h1, 4), across(h2, 2)
    parts = [(0, 0, part, own, 0), (1, 0, part, other, 0), (2, 0, part, got[2], 0)]
    parts += [(3, 0, part, got[3], 0), (4, 0, part, got[4], 0), (5, 0, part, got[5], 0)]
    schur, rows, ab = change([fresh(0, col[0]), fresh(1, col[1])], parts, cut(parts), schur, None, keeps=True, gives=True)
    d_op, schur = barrier((d_op, schur))
    d_late = send(d_op, {to: move for to, move in rounds[3].items() if is_late(to)})
    schur, rows, cc = change([fresh(2, c)], [], stored(6 * per), schur, rows, needed=below_at, gives=True)
    h1, h2, schur = barrier((h1, h2, schur))
    f1, f2 = across(h1, 1), across(h2, 1)
    far = [(6, 0, h, h1, 0), (6, h, h, h2, 0), (7, 0, h, f1, 0), (7, h, h, f2, 0)]
    beside = [p for p in parts if p[0] in (2, 3)]
    pieces = [(piece_at + m, None, None, (), (ab, m)) for m in (0, 1)]
    pieces += [fresh(2, ready=(cc, 0)), fresh(3, d_early, d_late)]
    schur, _ = change(pieces, far + beside, stored(6 * per) + cut(far), schur, rows, near=6 * per)
    return (diag_factor, panel_factor, schur)


def solution(mesh):
    nrow, ncol = mesh.shape["row"], mesh.shape["col"]
    return jax.shard_map(
        functools.partial(local, nrow, ncol),
        mesh=mesh,
        in_specs=(P(), P(("row", "col"), None), P("row", "col"), P("row", "col")),
        out_specs=(P(), P(("row", "col"), None), P("row", "col")),
        check_vma=False,
    )
```

```python
import functools

import jax
import jax.numpy as jnp
import numpy as np
from jax import lax
from jax.experimental import pallas as pl
from jax.experimental.pallas import tpu as pltpu
from jax.sharding import PartitionSpec as P

BLOCK = 256
T = 128
HIGHEST = lax.Precision.HIGHEST
AXES = ("row", "col")
F32, BF16 = jnp.float32, jnp.bfloat16


def tdot(a, b, precision=HIGHEST):
    return lax.dot_general(a, b, (((0,), (0,)), ((), ())), precision=precision, preferred_element_type=F32)


def split2(x):
    hi = x.astype(BF16)
    return hi, (x - hi.astype(F32)).astype(BF16)


def gram8(p):
    h = p.astype(BF16).astype(F32)
    m = (p - h).astype(BF16).astype(F32)
    l = p - h - m
    a = jnp.concatenate([h, h, m, m, h, l], 0).astype(BF16)
    b = jnp.concatenate([h, m, h, m, l, h], 0).astype(BF16)
    return tdot(a, b, None)


def factor_block(d):
    n = len(d)
    lane = lax.broadcasted_iota(jnp.int32, (8, T), 1)
    sub = lax.broadcasted_iota(jnp.int32, (8, T), 0)
    ws, us = [], []
    for g in range(n):
        e = d[g]
        cs = [jnp.broadcast_to(e[:, 8 * g + k : 8 * g + k + 1], (8, T)) for k in range(8)]
        inside = (lane >= 8 * g) & (lane < 8 * g + 8)
        e = jnp.where(inside, jnp.where(lane - 8 * g == sub, 1.0, 0.0), e)
        piv = jnp.ones((8, T), F32)
        for j in range(8):
            p = jnp.broadcast_to(cs[j][j : j + 1], (8, T))
            piv = jnp.where(sub == j, p, piv)
            if j == 7:
                break
            m = jnp.where(sub > j, cs[j] * (1.0 / p), 0.0)
            for k in range(j + 1, 8):
                cs[k] = cs[k] - m * jnp.broadcast_to(cs[k][j : j + 1], (8, T))
            e = e - m * jnp.broadcast_to(e[j : j + 1], (8, T))
        r = lax.rsqrt(piv)
        r = r * (1.5 - 0.5 * piv * r * r)
        e = e * r
        u = jnp.zeros((8, T), F32)
        for k in range(8):
            u = jnp.where((lane == 8 * g + k) & (sub <= k), cs[k] * r, u)
        us.append(jnp.where(lane >= 8 * g + 8, e, u))
        ws.append(jnp.where(lane < 8 * g + 8, e, 0.0))
        if g + 1 < n:
            update = gram8(e)
            for i in range(g + 1, n):
                d[i] = jnp.where(inside, 0.0, d[i]) - update[8 * i : 8 * i + 8]
    return ws, us


def factor_kernel(a_ref, old_ref, l_ref, inv_ref, new_ref, s_ref, w_ref, u_ref, p_ref, stage, sem):
    n = a_ref.shape[0]
    nb = n // T
    share = old_ref.shape[0] // nb

    def load(b):
        rows = pl.ds(pl.multiple_of(b * share, share), share)
        return pltpu.make_async_copy(old_ref.at[rows], stage.at[lax.rem(b, 2)], sem.at[lax.rem(b, 2)])

    def store(b):
        rows = pl.ds(pl.multiple_of(b * share, share), share)
        return pltpu.make_async_copy(stage.at[lax.rem(b, 2)], new_ref.at[rows], sem.at[2 + lax.rem(b, 2)])

    load(0).start()
    s_ref[...] = a_ref[...]
    l_ref[...] = jnp.zeros_like(l_ref)
    inv_ref[...] = jnp.zeros_like(inv_ref)
    colb = lax.broadcasted_iota(jnp.int32, (T, n), 1) // T

    @pl.loop(0, nb)
    def _(b):
        load(b).wait()
        store(b).start()

        @pl.when(b + 1 < nb)
        def _():
            @pl.when(b >= 1)
            def _():
                store(b - 1).wait()

            load(b + 1).start()

        here = pl.ds(pl.multiple_of(b * T, T), T)
        block = s_ref[here, here]
        ws, us = factor_block([block[8 * g : 8 * g + 8] for g in range(T // 8)])
        for g in range(T // 8):
            w_ref[8 * g : 8 * g + 8, :] = ws[g]
            u_ref[8 * g : 8 * g + 8, :] = us[g]
        w = w_ref[...]
        p_ref[...] = jnp.dot(w, s_ref[here, :], precision=HIGHEST, preferred_element_type=F32)
        p_ref[:, here] = w
        inv_ref[here, :] = jnp.where(colb <= b, p_ref[...], 0.0)
        l_ref[here, here] = u_ref[...].T

        @pl.loop(b + 1, nb)
        def _(i):
            there = pl.ds(pl.multiple_of(i * T, T), T)
            ui = p_ref[:, there]
            s_ref[there, :] = jnp.where(colb == b, 0.0, s_ref[there, :]) - tdot(ui, p_ref[...])
            l_ref[there, here] = ui.T

    if nb > 1:
        store(nb - 2).wait()
    store(nb - 1).wait()


VMEM = pl.BlockSpec(memory_space=pltpu.VMEM)
ANY = pl.BlockSpec(memory_space=pl.ANY)
BIG = pltpu.CompilerParams(vmem_limit_bytes=63 << 20)


def cost(flops, moved):
    return pl.CostEstimate(flops=int(flops), bytes_accessed=int(moved), transcendentals=0)


def factor(a, old):
    n = a.shape[0]
    full = jax.ShapeDtypeStruct((n, n), F32)
    return pl.pallas_call(
        factor_kernel,
        out_shape=(full, full, jax.ShapeDtypeStruct(old.shape, F32)),
        in_specs=[VMEM, ANY],
        out_specs=(VMEM, VMEM, ANY),
        scratch_shapes=[
            pltpu.VMEM((n, n), F32),
            pltpu.VMEM((T, T), F32),
            pltpu.VMEM((T, T), F32),
            pltpu.VMEM((T, n), F32),
            pltpu.VMEM((2, old.shape[0] * T // n, old.shape[1]), F32),
            pltpu.SemaphoreType.DMA((4,)),
        ],
        compiler_params=BIG,
        cost_estimate=cost(8e10, 12 << 20),
        name="factor",
    )(a, old)


def dot3(a_hi, a_lo, b_hi, b_lo):
    dot = functools.partial(jnp.dot, preferred_element_type=F32)
    return dot(a_hi, b_hi) + dot(a_lo, b_hi) + dot(a_hi, b_lo)


def inverse_kernel(inv_ref, rows_ref, x_ref, cat_ref, lt_hi, lt_lo, in_hi, in_lo, r_hi, r_lo):
    n = inv_ref.shape[0]

    @pl.loop(0, n // T)
    def _(k):
        part = pl.ds(pl.multiple_of(k * T, T), T)
        v = inv_ref[part, :]
        in_hi[part, :], in_lo[part, :] = split2(v)
        lt_hi[:, part], lt_lo[:, part] = split2(v.T)

    r_hi[...], r_lo[...] = split2(rows_ref[...])
    step = min(n, 256)
    for j in range(n // step):
        cols, deep = slice(j * step, (j + 1) * step), slice(0, (j + 1) * step)
        x_ref[:, cols] = dot3(r_hi[:, deep], r_lo[:, deep], lt_hi[deep, cols], lt_lo[deep, cols])
    for i in range(n // step):
        rows, deep = slice(i * step, (i + 1) * step), slice(i * step, n)
        cat_ref[rows, :], cat_ref[n + i * step : n + (i + 1) * step, :] = split2(dot3(lt_hi[rows, deep], lt_lo[rows, deep], in_hi[deep, :], in_lo[deep, :]))


def inverse(inv, rows):
    n, m = inv.shape[0], rows.shape[0]
    return pl.pallas_call(
        inverse_kernel,
        out_shape=(jax.ShapeDtypeStruct((m, n), F32), jax.ShapeDtypeStruct((2 * n, n), BF16)),
        in_specs=[VMEM] * 2,
        out_specs=(VMEM,) * 2,
        scratch_shapes=[pltpu.VMEM((n, n), BF16)] * 4 + [pltpu.VMEM((m, n), BF16)] * 2,
        compiler_params=BIG,
        cost_estimate=cost(8 * n * n * n, 16 << 20),
        name="inverse",
    )(inv, rows)


def pick_kernel(layout, info, *refs):
    arrays, outs, (buf, in_sem, out_sem) = refs[: layout["arrays"]], refs[layout["arrays"] : -3], refs[-3:]
    moves, at = [], 0
    for out, segments in zip(outs, layout["segments"]):
        for to, size, choices, entry in segments:
            moves.append((out, to, size, choices, entry, at))
            at += size
    for wait in (False, True):
        for number, (out, to, size, choices, entry, at) in enumerate(moves):
            stage = buf.at[pl.ds(at, size)]
            store = pltpu.make_async_copy(stage, out.at[pl.ds(to, size)], out_sem.at[number])
            for n, (frm, off) in enumerate(choices):
                load = pltpu.make_async_copy(arrays[frm].at[pl.ds(off, size)], stage, in_sem.at[number])

                @pl.when(True if entry is None else info[entry] == n)
                def _(load=load, store=store):
                    if wait:
                        load.wait()
                        store.start()
                    else:
                        load.start()
    for number, (out, to, size, choices, entry, at) in enumerate(moves):
        store = pltpu.make_async_copy(buf.at[pl.ds(at, size)], out.at[pl.ds(to, size)], out_sem.at[number])

        @pl.when(True if entry is None else info[entry] >= 0)
        def _(store=store):
            store.wait()


def pick(info, arrays, segments):
    cols = arrays[0].shape[1]
    count = sum(map(len, segments))
    return pl.pallas_call(
        functools.partial(pick_kernel, dict(arrays=len(arrays), segments=segments)),
        out_shape=tuple(jax.ShapeDtypeStruct((sum(s[1] for s in seg), cols), F32) for seg in segments),
        grid_spec=pltpu.PrefetchScalarGridSpec(
            num_scalar_prefetch=1,
            grid=(1,),
            in_specs=[ANY] * len(arrays),
            out_specs=(ANY,) * len(segments),
            scratch_shapes=[
                pltpu.VMEM((sum(s[1] for seg in segments for s in seg), cols), F32),
                pltpu.SemaphoreType.DMA((count,)),
                pltpu.SemaphoreType.DMA((count,)),
            ],
        ),
        compiler_params=BIG,
        cost_estimate=cost(1000, 1000),
        name="pick",
    )(info, *arrays)


AHEAD, RING, SLOTS, GROUP = 4, 12, 4, 4


def update_kernel(layout, info, pattern, *refs):
    pieces, parts, tiles = (layout[k] for k in ("pieces", "parts", "tiles"))
    tile, sub, part, ends = (layout[k] for k in ("tile", "sub", "part", "ends"))
    keeps_rows, gives, near = layout["keeps_rows"], layout["gives"], layout["near"]
    refs = list(refs)
    take = lambda k: [refs.pop(0) for _ in range(k)]
    sources = [take(p["sources"]) for p in pieces]
    ready = [take(1)[0] if p["ready"] is not None else None for p in pieces]
    part_refs, cat_ref = take(len(parts)), take(1)[0]
    take(1 + layout["rows_in"])
    out, rows_hbm, given = take(1)[0], (take(layout["rows_any"]) or [None])[0], (take(1 if gives else 0) or [None])[0]
    cat, p_buf, ht, row_f32, rows_v, block, flat, sem, p_sem, ht_sem, f32_sem, row_sem, in_sem, out_sem = refs
    count, steps = len(pieces), len(tiles)
    buffer = [sum(p["fresh"] for p in pieces[:m]) for m in range(count)]
    width, n = p_buf.shape[1:]
    subs = width // sub
    each = count * subs
    rb, cb = out.shape[0] // BLOCK, out.shape[1] // BLOCK
    r, c, diag, again = info[0], info[1], info[3] == 1, info[layout["again"]] == 1

    def row_of(step):
        at = step * tile
        return (jnp.bitwise_xor(at // part, c) * part) + at % part

    def col_of(m, s):
        q = info[pieces[0]["number"]]
        for k in range(1, count):
            q = jnp.where(m == k, info[pieces[k]["number"]], q)
        return q * width + s * sub

    def place(t):
        e = flat[t]
        return e // each, (e % each) // subs, e % subs

    def view(t):
        step, m, s = place(t)
        row, col = pl.multiple_of(row_of(step), tile), pl.multiple_of(col_of(m, s), sub)
        return out.at[pl.ds(row, tile), pl.ds(col, sub)]

    def load(t):
        return pltpu.make_async_copy(view(t), block.at[lax.rem(t, RING)], in_sem.at[lax.rem(t, RING)])

    def store(t):
        return pltpu.make_async_copy(block.at[lax.rem(t, RING)], view(t), out_sem.at[lax.rem(t, RING)])

    def prefetch(t, total):
        @pl.when(t < total)
        def _():
            @pl.when(t >= RING)
            def _():
                store(t - RING).wait()

            load(t).start()

    def every(copies, what):
        for yes, copy in copies:
            if yes is True:
                getattr(copy, what)()
            else:
                @pl.when(yes)
                def _(copy=copy):
                    getattr(copy, what)()

    @pl.when(info[layout["needed"]] == 1)
    def _():
        copy = pltpu.make_async_copy
        cats = [(True, copy(cat_ref, cat, sem.at[0]))]
        loads = [[] for _ in pieces]
        for m, p in enumerate(pieces):
            for k in range(p["sources"]):
                chosen = (info[p["where"]] == k) if p["sources"] > 1 else True
                loads[m].append((jnp.logical_not(diag) & chosen, copy(sources[m][k], p_buf.at[buffer[m]], p_sem.at[m, k])))
            if p["fresh"]:
                for k, (mask, off, size, frm) in enumerate(parts):
                    to = p_buf.at[buffer[m], pl.ds(off, size)]
                    loads[m].append((diag & (info[p["mask"]] == mask), copy(part_refs[k].at[pl.ds(frm, size)], to, p_sem.at[m, 2 + k])))
        hts = []
        for m, p in enumerate(pieces):
            if p["ready"] is not None:
                src = ready[m].at[pl.ds(p["ready"] * width, width)]
                yes = jnp.logical_not(again) if p["fresh"] else True
                hts.append((yes, copy(src, ht.at[m], ht_sem.at[m])))
        stored = [t for t, (k, _) in enumerate(tiles) if k is None]
        floats = [t for t, (k, _) in enumerate(tiles) if k is not None]
        rows = [(True, copy(rows_hbm.at[pl.ds(t * tile, tile)], rows_v.at[pl.ds(t * tile, tile)], row_sem.at[t])) for t in stored]

        def float_copy(u):
            k, off = tiles[floats[u]]
            return copy(part_refs[k].at[pl.ds(off, tile)], row_f32.at[u % SLOTS], f32_sem.at[u % SLOTS])

        def keep_copy(u):
            here = pl.ds(floats[u] * tile, tile)
            return copy(rows_v.at[here], rows_hbm.at[here], row_sem.at[floats[u]])

        for m in range(count):
            every(loads[m], "start")
        every(cats, "start")

        def note(e, found):
            step, m, s = e // each, (e % each) // subs, e % subs
            row, col = row_of(step) // BLOCK, col_of(m, s) // BLOCK
            flat[found] = e
            kept = (pattern[row, col] == 1) & (r * rb + row >= c * cb + col)
            if near:
                now = step >= near
                for k, p in enumerate(pieces):
                    now = now | ((m == k) & (again if p["ready"] is not None else True)) if p["fresh"] else now
                kept = kept & now
            return found + kept.astype(jnp.int32)

        counts = [0]
        for start, end in zip([0] + ends, ends):
            counts.append(lax.fori_loop(start * each, end * each, note, counts[-1]))
        total = counts[-1]
        for t in range(AHEAD):
            prefetch(t, total)

        def split_tile(u):
            float_copy(u).wait()
            here = pl.ds(floats[u] * tile, tile)
            rows_v[here, :n], rows_v[here, n:] = split2(row_f32[u % SLOTS])
            if u + SLOTS < len(floats):
                float_copy(u + SLOTS).start()
            if keeps_rows:
                keep_copy(u).start()

        step = min(width, 256)
        chunks = [(m, at) for m, p in enumerate(pieces) if p["fresh"] for at in range(0, width, step)]
        gone = []
        for number, (m, at) in enumerate(chunks):
            if at == 0:
                every(loads[m], "wait")
            if number == 0:
                every(cats, "wait")
                for u in range(min(SLOTS, len(floats))):
                    float_copy(u).start()
                every(rows, "start")
                every(hts, "start")
            here = slice(at, at + step)

            def multiply(m=m, here=here):
                hi, lo = split2(p_buf[buffer[m], here])
                ht[m, here, :n], ht[m, here, n:] = split2(dot3(hi, lo, cat[:n], cat[n:]))

            if pieces[m]["ready"] is None:
                multiply()
            else:
                pl.when(again)(multiply)
            if gives and at + step == width:
                gone.append((True, copy(ht.at[m], given.at[pl.ds(m * width, width)], sem.at[1 + m])))
                every(gone[-1:], "start")
            early = [u for u in range(len(floats)) if floats[u] < ends[0]]
            for u in early:
                if u * len(chunks) // len(early) == number:
                    split_tile(u)

        def product(t):
            tile_at, m, s = place(t)
            mine = rows_v[pl.ds(pl.multiple_of(tile_at * tile, tile), tile), :]
            cols = pl.ds(pl.multiple_of(s * sub, sub), sub)
            dot = functools.partial(lax.dot_general, dimension_numbers=(((1,), (1,)), ((), ())), preferred_element_type=F32)
            return dot(mine[:, :n], ht[m, cols, :n]) + dot(mine[:, n:], ht[m, cols, :n]) + dot(mine[:, :n], ht[m, cols, n:])

        def finish(t, value):
            load(t).wait()
            block[lax.rem(t, RING)] = block[lax.rem(t, RING)] - value
            store(t).start()

        def work(t, size):
            for k in range(size):
                prefetch(t + k + AHEAD, total)
            values = [product(t + k) for k in range(size)]
            for k in range(size):
                finish(t + k, values[k])

        for k, (start, end) in enumerate(zip([0] + ends, ends)):
            every([rows[j] for j, t in enumerate(stored) if start <= t < end], "wait")
            if k == len(ends) - 1:
                every(hts, "wait")
            if k:
                for u in range(len(floats)):
                    if start <= floats[u] < end:
                        split_tile(u)
            whole = counts[k] + (counts[k + 1] - counts[k]) // GROUP * GROUP

            @pl.loop(counts[k], whole, step=GROUP)
            def _(t):
                work(t, GROUP)

            @pl.loop(whole, counts[k + 1])
            def _(t):
                work(t, 1)

        @pl.loop(jnp.maximum(total - RING, 0), total)
        def _(t):
            store(t).wait()

        every(gone, "wait")
        if keeps_rows:
            for u in range(len(floats)):
                keep_copy(u).wait()


def update(info, pattern, pieces, parts, tiles, ends, near, needed, again, tile, part, cat, schur, rows, keeps_rows, gives):
    n = cat.shape[1]
    width = next(p[3][0].shape[0] for p in pieces if p[3])
    local_rows, local_cols = schur.shape
    sub = min(width, BLOCK)
    count, steps = len(pieces), len(tiles)
    layout = dict(
        pieces=[
            dict(number=a, mask=b, where=w, sources=len(x), ready=None if y is None else y[1], fresh=b is not None)
            for a, b, w, x, y in pieces
        ],
        parts=[(mask, off, size, frm) for mask, off, size, _, frm in parts],
        tiles=tiles,
        ends=ends,
        near=near,
        needed=needed,
        again=again,
        tile=tile,
        sub=sub,
        part=part,
        keeps_rows=keeps_rows,
        gives=gives,
        rows_in=0 if rows is None else 1,
        rows_any=1 if keeps_rows or rows is not None else 0,
    )
    operands = [x for p in pieces for x in p[3]] + [p[4][0] for p in pieces if p[4] is not None] + [p[3] for p in parts] + [cat, schur]
    aliases = {2 + len(operands) - 1: 0}
    shapes = [jax.ShapeDtypeStruct(schur.shape, F32)]
    if rows is not None:
        operands.append(rows)
        aliases[2 + len(operands) - 1] = 1
    if layout["rows_any"]:
        shapes.append(jax.ShapeDtypeStruct((local_rows, 2 * n), BF16))
    if gives:
        shapes.append(jax.ShapeDtypeStruct((count * width, 2 * n), BF16))
    dma = pltpu.SemaphoreType.DMA
    return pl.pallas_call(
        functools.partial(update_kernel, layout),
        out_shape=tuple(shapes),
        grid_spec=pltpu.PrefetchScalarGridSpec(
            num_scalar_prefetch=2,
            grid=(1,),
            in_specs=[ANY] * len(operands),
            out_specs=(ANY,) * len(shapes),
            scratch_shapes=[
                pltpu.VMEM((2 * n, n), BF16),
                pltpu.VMEM((sum(p["fresh"] for p in layout["pieces"]), width, n), F32),
                pltpu.VMEM((count, width, 2 * n), BF16),
                pltpu.VMEM((SLOTS, tile, n), F32),
                pltpu.VMEM((steps * tile, 2 * n), BF16),
                pltpu.VMEM((RING, tile, sub), F32),
                pltpu.SMEM((steps * count * (width // sub) + 1,), jnp.int32),
                dma((2 + count,)),
                dma((count, 2 + len(parts))),
                dma((count,)),
                dma((SLOTS,)),
                dma((steps,)),
                dma((RING,)),
                dma((RING,)),
            ],
        ),
        input_output_aliases=aliases,
        compiler_params=BIG,
        cost_estimate=cost(1000, 1000),
        name="update",
    )(info, pattern, *operands)


def plan(nrow, ncol):
    half, ratio = nrow // 2, ncol // nrow
    if (nrow, ncol) != (4, 8):
        shift = {nrow - 1: 0, nrow - 2: half}
        free = [g for g in range(1, nrow) if g != half]
        for i in range(nrow - 2):
            shift[i] = free[i]
        rounds = [{} for _ in range(nrow)]
        for m in range(nrow):
            for i in range(nrow):
                for j in range(i * ratio):
                    q = m ^ shift[i]
                    rounds[m][i, j] = (divmod(j * nrow + q, ncol), "own", q)
        return rounds
    rounds = [{} for _ in range(4)]

    def at(z, y, x, k):
        return z, (y * 2 + x) * 2 + k

    def put(m, to, frm, kind, x, k):
        rounds[m][at(*to)] = (at(*frm), kind, 2 * x + k)

    first = {0: (0, 1), 1: (0, 0), 2: (1, 0)}
    for z in (1, 2, 3):
        for src in range(z):
            y, x = divmod(src, 2)
            for core in (0, 1):
                half_x = first[src][core] if z != 2 else 1 - first[src][core]
                for m in (0, 1):
                    k = m if z != 1 else 1 - m
                    put(m, (z, y, x, core), (src, core, half_x, k), "own", half_x, k)
    put(2, (3, 0, 0, 0), (0, 0, 0, 0), "x", 1, 0)
    put(2, (3, 0, 0, 1), (0, 0, 0, 1), "y", 0, 1)
    put(3, (3, 0, 0, 0), (0, 0, 0, 1), "x", 1, 1)
    put(3, (3, 0, 0, 1), (0, 1, 1, 0), "x", 0, 0)
    put(2, (3, 0, 1, 0), (1, 0, 1, 0), "own", 1, 0)
    put(2, (3, 0, 1, 1), (1, 0, 1, 1), "y", 1, 1)
    put(3, (3, 0, 1, 0), (1, 0, 1, 1), "own", 1, 1)
    put(3, (3, 0, 1, 1), (1, 1, 1, 0), "own", 1, 0)
    put(2, (3, 1, 0, 1), (2, 1, 0, 0), "x", 1, 0)
    put(2, (3, 1, 0, 0), (2, 1, 0, 1), "y", 0, 1)
    put(3, (3, 1, 0, 1), (2, 1, 1, 1), "own", 1, 1)
    put(3, (3, 1, 0, 0), (2, 1, 0, 0), "y", 0, 0)
    put(2, (2, 0, 0, 0), (3, 0, 0, 0), "a", 0, 0)
    put(3, (2, 0, 0, 0), (3, 0, 0, 0), "b", 0, 1)
    put(2, (2, 0, 0, 1), (3, 0, 0, 1), "a", 1, 0)
    put(3, (2, 0, 0, 1), (0, 1, 1, 1), "own", 1, 1)
    put(2, (2, 0, 1, 0), (3, 0, 1, 0), "a", 0, 0)
    put(3, (2, 0, 1, 0), (3, 0, 1, 0), "b", 0, 1)
    put(2, (2, 0, 1, 1), (3, 0, 1, 1), "a", 0, 0)
    put(3, (2, 0, 1, 1), (1, 1, 0, 1), "own", 0, 1)
    for m in (2, 3):
        put(m, (1, 0, 0, 0), (0, 0, 1, m - 2), "own", 1, m - 2)
        put(m, (1, 0, 0, 1), (0, 1, 0, m - 2), "own", 0, m - 2)
    return rounds


KINDS = ("own", "x", "y", "a", "b")


def tables(nrow, ncol, rounds):
    ratio = ncol // nrow
    tight, half = (nrow, ncol) == (4, 8), nrow // 2
    out = []
    for i in range(nrow):
        for j in range(ncol):
            qs = []
            for m in range(nrow):
                if (i, j) in rounds[m]:
                    qs.append(rounds[m][i, j][2])
                elif tight:
                    qs.append(m ^ (2 * ((j >> 1) & 1)))
                else:
                    qs.append(m)
            masks = [((j * nrow + q) % ncol) ^ j for q in qs]
            sent = [-1] * nrow
            for m in range(nrow):
                for (frm, kind, _) in rounds[m].values():
                    if frm == (i, j):
                        sent[m] = KINDS.index(kind)
            late = int(tight and is_late((i, j)))
            again = int(i == j // ratio and masks[half] > 5)
            out.append([i, j, int(i >= j // ratio), int(i == j // ratio), *qs, *masks, *sent, late, int(i > j // ratio or (i == j // ratio and not again)), again])
    return np.array(out, np.int32)


def is_late(to):
    return to in ((3, 0), (3, 2), (3, 4))


def local(nrow, ncol, front_diag, panel_rows, trailing, pattern):
    local_rows = trailing.shape[0]
    part = panel_rows.shape[0]
    half = nrow // 2
    everyone = [(i, j) for i in range(nrow) for j in range(ncol)]
    rounds = plan(nrow, ncol)
    info = jnp.asarray(tables(nrow, ncol, rounds))[lax.axis_index("row") * ncol + lax.axis_index("col")]
    piece_at, mask_at, sent_at, late_at = 4, 4 + nrow, 4 + 2 * nrow, 4 + 3 * nrow
    barrier = lax.optimization_barrier

    def across(x, mask):
        return lax.ppermute(x, AXES, [(i * ncol + j, i * ncol + (j ^ mask)) for i, j in everyone])

    def send(x, moves):
        return lax.ppermute(x, AXES, [(a * ncol + b, i * ncol + j) for (i, j), ((a, b), _, _) in moves.items()])

    tight = (nrow, ncol) == (4, 8)
    tile = min(BLOCK, part // 2 if tight else part)
    per = part // tile
    below_at = late_at + 1

    def fresh(m, *sources, ready=None):
        return piece_at + m, mask_at + m, late_at, sources, ready

    def cut(parts):
        return [(k, frm + s) for k, (_, _, size, _, frm) in enumerate(parts) for s in range(0, size, tile)]

    def stored(steps):
        return [(None, t * tile) for t in range(steps)]

    def change(pieces, parts, tiles, s, rows, near=0, needed=2, keeps=False, gives=False, ends=None):
        return update(info, pattern, pieces, parts, tiles, ends or [len(tiles)], near, needed, below_at + 1, tile, part, cat, s, rows, keeps, gives)

    near = [m for m in range(2, ncol, 2) if not (tight and m == 6)]
    got = {m: across(panel_rows, m) for m in near}
    col = [send(panel_rows, rounds[m]) for m in range(half)]
    other = across(panel_rows, 1)
    front_diag, info = barrier((front_diag, info))
    diag_factor, inv, schur = factor(front_diag, trailing)
    panel_factor, cat = inverse(inv, panel_rows)
    held, cat = barrier(([panel_rows, other, *[got[m] for m in near], *col], cat))
    own, other, got, col = held[0], held[1], dict(zip(near, held[2:])), held[2 + len(near) :]

    if not tight:
        parts = [(0, 0, part, own, 0), (1, 0, part, other, 0)]
        for m in near:
            parts += [(m, 0, part, got[m], 0), (m + 1, 0, part, across(got[m], 1), 0)]
        col = [*col, *[send(own, rounds[m]) for m in range(half, nrow)]]
        parts.sort(key=lambda p: p[0])
        one, two = [[fresh(m, col[m]) for m in ms] for ms in (range(half), range(half, nrow))]
        schur, rows = change(one, parts, cut(parts), schur, None, keeps=True)
        schur, _ = change(two, parts, stored(ncol * per), schur, rows)
        return (diag_factor, panel_factor, schur)

    h = part // 2
    arrays = [own, got[2], got[4], col[0], col[1]]
    choices = [(k, 0) for k in range(5)]
    c_op, d_op, h1, h2 = pick(
        info,
        arrays,
        [
            [(0, part, choices, sent_at + 2)],
            [(0, part, choices, sent_at + 3)],
            [(0, h, [(1, 0)], None)],
            [(0, h, [(2, h)], None)],
        ],
    )
    c = send(c_op, rounds[2])
    d_early = send(d_op, {to: move for to, move in rounds[3].items() if not is_late(to)})
    got[3], got[5] = across(got[2], 1), across(got[4], 1)
    h1, h2 = across(h1, 4), across(h2, 2)
    parts = [(0, 0, part, own, 0), (1, 0, part, other, 0), (2, 0, part, got[2], 0)]
    parts += [(3, 0, part, got[3], 0), (4, 0, part, got[4], 0), (5, 0, part, got[5], 0)]
    schur, rows, ab = change([fresh(0, col[0]), fresh(1, col[1])], parts, cut(parts), schur, None, keeps=True, gives=True)
    d_op, schur = barrier((d_op, schur))
    d_late = send(d_op, {to: move for to, move in rounds[3].items() if is_late(to)})
    beside = [p for p in parts if p[0] in (2, 3)]
    schur, rows, cc = change([fresh(2, c)], beside, stored(6 * per), schur, rows, needed=below_at, gives=True, ends=[3 * per, 6 * per])
    h1, h2, schur = barrier((h1, h2, schur))
    f1, f2 = across(h1, 1), across(h2, 1)
    far = [(6, 0, h, h1, 0), (6, h, h, h2, 0), (7, 0, h, f1, 0), (7, h, h, f2, 0)]
    pieces = [(piece_at + m, None, None, (), (ab, m)) for m in (0, 1)]
    pieces += [fresh(2, ready=(cc, 0)), fresh(3, d_early, d_late)]
    schur, _ = change(pieces, far + beside, stored(6 * per) + cut(far), schur, rows, near=6 * per, ends=[3 * per, 6 * per, 8 * per])
    return (diag_factor, panel_factor, schur)


def solution(mesh):
    nrow, ncol = mesh.shape["row"], mesh.shape["col"]
    return jax.shard_map(
        functools.partial(local, nrow, ncol),
        mesh=mesh,
        in_specs=(P(), P(("row", "col"), None), P("row", "col"), P("row", "col")),
        out_specs=(P(), P(("row", "col"), None), P("row", "col")),
        check_vma=False,
    )
```

```python
import functools

import jax
import jax.numpy as jnp
import numpy as np
from jax import lax
from jax.experimental import pallas as pl
from jax.experimental.pallas import tpu as pltpu
from jax.sharding import PartitionSpec as P

BLOCK = 256
T = 128
HIGHEST = lax.Precision.HIGHEST
AXES = ("row", "col")
F32, BF16 = jnp.float32, jnp.bfloat16


def tdot(a, b, precision=HIGHEST):
    return lax.dot_general(a, b, (((0,), (0,)), ((), ())), precision=precision, preferred_element_type=F32)


def split2(x):
    hi = x.astype(BF16)
    return hi, (x - hi.astype(F32)).astype(BF16)


def gram8(p):
    h = p.astype(BF16).astype(F32)
    m = (p - h).astype(BF16).astype(F32)
    l = p - h - m
    a = jnp.concatenate([h, h, m, m, h, l], 0).astype(BF16)
    b = jnp.concatenate([h, m, h, m, l, h], 0).astype(BF16)
    return tdot(a, b, None)


def factor_block(d):
    n = len(d)
    lane = lax.broadcasted_iota(jnp.int32, (8, T), 1)
    sub = lax.broadcasted_iota(jnp.int32, (8, T), 0)
    ws, us = [], []
    for g in range(n):
        e = d[g]
        cs = [jnp.broadcast_to(e[:, 8 * g + k : 8 * g + k + 1], (8, T)) for k in range(8)]
        inside = (lane >= 8 * g) & (lane < 8 * g + 8)
        e = jnp.where(inside, jnp.where(lane - 8 * g == sub, 1.0, 0.0), e)
        piv = jnp.ones((8, T), F32)
        for j in range(8):
            p = jnp.broadcast_to(cs[j][j : j + 1], (8, T))
            piv = jnp.where(sub == j, p, piv)
            if j == 7:
                break
            m = jnp.where(sub > j, cs[j] * (1.0 / p), 0.0)
            for k in range(j + 1, 8):
                cs[k] = cs[k] - m * jnp.broadcast_to(cs[k][j : j + 1], (8, T))
            e = e - m * jnp.broadcast_to(e[j : j + 1], (8, T))
        r = lax.rsqrt(piv)
        r = r * (1.5 - 0.5 * piv * r * r)
        e = e * r
        u = jnp.zeros((8, T), F32)
        for k in range(8):
            u = jnp.where((lane == 8 * g + k) & (sub <= k), cs[k] * r, u)
        us.append(jnp.where(lane >= 8 * g + 8, e, u))
        ws.append(jnp.where(lane < 8 * g + 8, e, 0.0))
        if g + 1 < n:
            update = gram8(e)
            for i in range(g + 1, n):
                d[i] = jnp.where(inside, 0.0, d[i]) - update[8 * i : 8 * i + 8]
    return ws, us


def factor_kernel(a_ref, old_ref, l_ref, inv_ref, new_ref, s_ref, w_ref, u_ref, p_ref, stage, sem):
    n = a_ref.shape[0]
    nb = n // T
    share = old_ref.shape[0] // nb

    def load(b):
        rows = pl.ds(pl.multiple_of(b * share, share), share)
        return pltpu.make_async_copy(old_ref.at[rows], stage.at[lax.rem(b, 2)], sem.at[lax.rem(b, 2)])

    def store(b):
        rows = pl.ds(pl.multiple_of(b * share, share), share)
        return pltpu.make_async_copy(stage.at[lax.rem(b, 2)], new_ref.at[rows], sem.at[2 + lax.rem(b, 2)])

    load(0).start()
    s_ref[...] = a_ref[...]
    l_ref[...] = jnp.zeros_like(l_ref)
    inv_ref[...] = jnp.zeros_like(inv_ref)
    colb = lax.broadcasted_iota(jnp.int32, (T, n), 1) // T

    @pl.loop(0, nb)
    def _(b):
        load(b).wait()
        store(b).start()

        @pl.when(b + 1 < nb)
        def _():
            @pl.when(b >= 1)
            def _():
                store(b - 1).wait()

            load(b + 1).start()

        here = pl.ds(pl.multiple_of(b * T, T), T)
        block = s_ref[here, here]
        ws, us = factor_block([block[8 * g : 8 * g + 8] for g in range(T // 8)])
        for g in range(T // 8):
            w_ref[8 * g : 8 * g + 8, :] = ws[g]
            u_ref[8 * g : 8 * g + 8, :] = us[g]
        w = w_ref[...]
        p_ref[...] = jnp.dot(w, s_ref[here, :], precision=HIGHEST, preferred_element_type=F32)
        p_ref[:, here] = w
        inv_ref[here, :] = jnp.where(colb <= b, p_ref[...], 0.0)
        l_ref[here, here] = u_ref[...].T

        @pl.loop(b + 1, nb)
        def _(i):
            there = pl.ds(pl.multiple_of(i * T, T), T)
            ui = p_ref[:, there]
            s_ref[there, :] = jnp.where(colb == b, 0.0, s_ref[there, :]) - tdot(ui, p_ref[...])
            l_ref[there, here] = ui.T

    if nb > 1:
        store(nb - 2).wait()
    store(nb - 1).wait()


VMEM = pl.BlockSpec(memory_space=pltpu.VMEM)
ANY = pl.BlockSpec(memory_space=pl.ANY)
BIG = pltpu.CompilerParams(vmem_limit_bytes=63 << 20)


def cost(flops, moved):
    return pl.CostEstimate(flops=int(flops), bytes_accessed=int(moved), transcendentals=0)


def factor(a, old):
    n = a.shape[0]
    full = jax.ShapeDtypeStruct((n, n), F32)
    return pl.pallas_call(
        factor_kernel,
        out_shape=(full, full, jax.ShapeDtypeStruct(old.shape, F32)),
        in_specs=[VMEM, ANY],
        out_specs=(VMEM, VMEM, ANY),
        scratch_shapes=[
            pltpu.VMEM((n, n), F32),
            pltpu.VMEM((T, T), F32),
            pltpu.VMEM((T, T), F32),
            pltpu.VMEM((T, n), F32),
            pltpu.VMEM((2, old.shape[0] * T // n, old.shape[1]), F32),
            pltpu.SemaphoreType.DMA((4,)),
        ],
        compiler_params=BIG,
        cost_estimate=cost(8e10, 12 << 20),
        name="factor",
    )(a, old)


def dot3(a_hi, a_lo, b_hi, b_lo):
    dot = functools.partial(jnp.dot, preferred_element_type=F32)
    return dot(a_hi, b_hi) + dot(a_lo, b_hi) + dot(a_hi, b_lo)


def inverse_kernel(inv_ref, rows_ref, x_ref, cat_ref, lt_hi, lt_lo, in_hi, in_lo, r_hi, r_lo):
    n = inv_ref.shape[0]

    @pl.loop(0, n // T)
    def _(k):
        part = pl.ds(pl.multiple_of(k * T, T), T)
        v = inv_ref[part, :]
        in_hi[part, :], in_lo[part, :] = split2(v)
        lt_hi[:, part], lt_lo[:, part] = split2(v.T)

    r_hi[...], r_lo[...] = split2(rows_ref[...])
    step = min(n, 256)
    for j in range(n // step):
        cols, deep = slice(j * step, (j + 1) * step), slice(0, (j + 1) * step)
        x_ref[:, cols] = dot3(r_hi[:, deep], r_lo[:, deep], lt_hi[deep, cols], lt_lo[deep, cols])
    for i in range(n // step):
        rows, deep = slice(i * step, (i + 1) * step), slice(i * step, n)
        cat_ref[rows, :], cat_ref[n + i * step : n + (i + 1) * step, :] = split2(dot3(lt_hi[rows, deep], lt_lo[rows, deep], in_hi[deep, :], in_lo[deep, :]))


def inverse(inv, rows):
    n, m = inv.shape[0], rows.shape[0]
    return pl.pallas_call(
        inverse_kernel,
        out_shape=(jax.ShapeDtypeStruct((m, n), F32), jax.ShapeDtypeStruct((2 * n, n), BF16)),
        in_specs=[VMEM] * 2,
        out_specs=(VMEM,) * 2,
        scratch_shapes=[pltpu.VMEM((n, n), BF16)] * 4 + [pltpu.VMEM((m, n), BF16)] * 2,
        compiler_params=BIG,
        cost_estimate=cost(8 * n * n * n, 16 << 20),
        name="inverse",
    )(inv, rows)


def pick_kernel(layout, info, *refs):
    arrays, outs, (buf, in_sem, out_sem) = refs[: layout["arrays"]], refs[layout["arrays"] : -3], refs[-3:]
    moves, at = [], 0
    for out, segments in zip(outs, layout["segments"]):
        for to, size, choices, entry in segments:
            moves.append((out, to, size, choices, entry, at))
            at += size
    for wait in (False, True):
        for number, (out, to, size, choices, entry, at) in enumerate(moves):
            stage = buf.at[pl.ds(at, size)]
            store = pltpu.make_async_copy(stage, out.at[pl.ds(to, size)], out_sem.at[number])
            for n, (frm, off) in enumerate(choices):
                load = pltpu.make_async_copy(arrays[frm].at[pl.ds(off, size)], stage, in_sem.at[number])

                @pl.when(True if entry is None else info[entry] == n)
                def _(load=load, store=store):
                    if wait:
                        load.wait()
                        store.start()
                    else:
                        load.start()
    for number, (out, to, size, choices, entry, at) in enumerate(moves):
        store = pltpu.make_async_copy(buf.at[pl.ds(at, size)], out.at[pl.ds(to, size)], out_sem.at[number])

        @pl.when(True if entry is None else info[entry] >= 0)
        def _(store=store):
            store.wait()


def pick(info, arrays, segments):
    cols = arrays[0].shape[1]
    count = sum(map(len, segments))
    return pl.pallas_call(
        functools.partial(pick_kernel, dict(arrays=len(arrays), segments=segments)),
        out_shape=tuple(jax.ShapeDtypeStruct((sum(s[1] for s in seg), cols), F32) for seg in segments),
        grid_spec=pltpu.PrefetchScalarGridSpec(
            num_scalar_prefetch=1,
            grid=(1,),
            in_specs=[ANY] * len(arrays),
            out_specs=(ANY,) * len(segments),
            scratch_shapes=[
                pltpu.VMEM((sum(s[1] for seg in segments for s in seg), cols), F32),
                pltpu.SemaphoreType.DMA((count,)),
                pltpu.SemaphoreType.DMA((count,)),
            ],
        ),
        compiler_params=BIG,
        cost_estimate=cost(1000, 1000),
        name="pick",
    )(info, *arrays)


AHEAD, RING, SLOTS, GROUP = 4, 12, 4, 4


def update_kernel(layout, info, pattern, *refs):
    pieces, parts, tiles = (layout[k] for k in ("pieces", "parts", "tiles"))
    tile, sub, part, ends = (layout[k] for k in ("tile", "sub", "part", "ends"))
    keeps_rows, gives, near = layout["keeps_rows"], layout["gives"], layout["near"]
    refs = list(refs)
    take = lambda k: [refs.pop(0) for _ in range(k)]
    sources = [take(p["sources"]) for p in pieces]
    ready = [take(1)[0] if p["ready"] is not None else None for p in pieces]
    part_refs, cat_ref = take(len(parts)), take(1)[0]
    take(1 + layout["rows_in"])
    out, rows_hbm, given = take(1)[0], (take(layout["rows_any"]) or [None])[0], (take(1 if gives else 0) or [None])[0]
    cat, p_buf, ht, row_f32, rows_v, block, flat, sem, p_sem, ht_sem, f32_sem, row_sem, in_sem, out_sem = refs
    count, steps = len(pieces), len(tiles)
    buffer = [sum(p["fresh"] for p in pieces[:m]) for m in range(count)]
    width, n = p_buf.shape[1:]
    subs = width // sub
    each = count * subs
    rb, cb = out.shape[0] // BLOCK, out.shape[1] // BLOCK
    r, c, diag, again = info[0], info[1], info[3] == 1, info[layout["again"]] == 1

    def row_of(step):
        at = step * tile
        return (jnp.bitwise_xor(at // part, c) * part) + at % part

    def col_of(m, s):
        q = info[pieces[0]["number"]]
        for k in range(1, count):
            q = jnp.where(m == k, info[pieces[k]["number"]], q)
        return q * width + s * sub

    def place(t):
        e = flat[t]
        return e // each, (e % each) // subs, e % subs

    def view(t):
        step, m, s = place(t)
        row, col = pl.multiple_of(row_of(step), tile), pl.multiple_of(col_of(m, s), sub)
        return out.at[pl.ds(row, tile), pl.ds(col, sub)]

    def load(t):
        return pltpu.make_async_copy(view(t), block.at[lax.rem(t, RING)], in_sem.at[lax.rem(t, RING)])

    def store(t):
        return pltpu.make_async_copy(block.at[lax.rem(t, RING)], view(t), out_sem.at[lax.rem(t, RING)])

    def prefetch(t, total):
        @pl.when(t < total)
        def _():
            @pl.when(t >= RING)
            def _():
                store(t - RING).wait()

            load(t).start()

    def every(copies, what):
        for yes, copy in copies:
            if yes is True:
                getattr(copy, what)()
            else:
                @pl.when(yes)
                def _(copy=copy):
                    getattr(copy, what)()

    @pl.when(info[layout["needed"]] == 1)
    def _():
        copy = pltpu.make_async_copy
        cats = [(True, copy(cat_ref, cat, sem.at[0]))]
        loads = [[] for _ in pieces]
        for m, p in enumerate(pieces):
            for k in range(p["sources"]):
                chosen = (info[p["where"]] == k) if p["sources"] > 1 else True
                loads[m].append((jnp.logical_not(diag) & chosen, copy(sources[m][k], p_buf.at[buffer[m]], p_sem.at[m, k])))
            if p["fresh"]:
                for k, (mask, off, size, frm) in enumerate(parts):
                    to = p_buf.at[buffer[m], pl.ds(off, size)]
                    loads[m].append((diag & (info[p["mask"]] == mask), copy(part_refs[k].at[pl.ds(frm, size)], to, p_sem.at[m, 2 + k])))
        hts = []
        for m, p in enumerate(pieces):
            if p["ready"] is not None:
                src = ready[m].at[pl.ds(p["ready"] * width, width)]
                yes = jnp.logical_not(again) if p["fresh"] else True
                hts.append((yes, copy(src, ht.at[m], ht_sem.at[m])))
        stored = [t for t, (k, _) in enumerate(tiles) if k is None]
        floats = [t for t, (k, _) in enumerate(tiles) if k is not None]
        rows = [(True, copy(rows_hbm.at[pl.ds(t * tile, tile)], rows_v.at[pl.ds(t * tile, tile)], row_sem.at[t])) for t in stored]

        def float_copy(u):
            k, off = tiles[floats[u]]
            return copy(part_refs[k].at[pl.ds(off, tile)], row_f32.at[u % SLOTS], f32_sem.at[u % SLOTS])

        def keep_copy(u):
            here = pl.ds(floats[u] * tile, tile)
            return copy(rows_v.at[here], rows_hbm.at[here], row_sem.at[floats[u]])

        for m in range(count):
            every(loads[m], "start")
        every(cats, "start")
        eager = [k for k, t in enumerate(stored) if near and t < ends[0]]
        every([rows[k] for k in eager], "start")

        def note(e, found):
            step, m, s = e // each, (e % each) // subs, e % subs
            row, col = row_of(step) // BLOCK, col_of(m, s) // BLOCK
            flat[found] = e
            kept = (pattern[row, col] == 1) & (r * rb + row >= c * cb + col)
            if near:
                now = step >= near
                for k, p in enumerate(pieces):
                    now = now | ((m == k) & (again if p["ready"] is not None else True)) if p["fresh"] else now
                kept = kept & now
            return found + kept.astype(jnp.int32)

        counts = [0]
        for start, end in zip([0] + ends, ends):
            counts.append(lax.fori_loop(start * each, end * each, note, counts[-1]))
        total = counts[-1]
        for t in range(AHEAD):
            prefetch(t, total)

        def split_tile(u):
            float_copy(u).wait()
            here = pl.ds(floats[u] * tile, tile)
            rows_v[here, :n], rows_v[here, n:] = split2(row_f32[u % SLOTS])
            if u + SLOTS < len(floats):
                float_copy(u + SLOTS).start()
            if keeps_rows:
                keep_copy(u).start()

        step = min(width, 256)
        chunks = [(m, at) for m, p in enumerate(pieces) if p["fresh"] for at in range(0, width, step)]
        gone = []
        for number, (m, at) in enumerate(chunks):
            if at == 0:
                every(loads[m], "wait")
            if number == 0:
                every(cats, "wait")
                for u in range(min(SLOTS, len(floats))):
                    float_copy(u).start()
                every([copies for k, copies in enumerate(rows) if k not in eager], "start")
                every(hts, "start")
            here = slice(at, at + step)

            def multiply(m=m, here=here):
                hi, lo = split2(p_buf[buffer[m], here])
                ht[m, here, :n], ht[m, here, n:] = split2(dot3(hi, lo, cat[:n], cat[n:]))

            if pieces[m]["ready"] is None:
                multiply()
            else:
                pl.when(again)(multiply)
            if gives and at + step == width:
                gone.append((True, copy(ht.at[m], given.at[pl.ds(m * width, width)], sem.at[1 + m])))
                every(gone[-1:], "start")
            early = [u for u in range(len(floats)) if floats[u] < ends[0]]
            for u in early:
                if u * len(chunks) // len(early) == number:
                    split_tile(u)

        def product(t):
            tile_at, m, s = place(t)
            mine = rows_v[pl.ds(pl.multiple_of(tile_at * tile, tile), tile), :]
            cols = pl.ds(pl.multiple_of(s * sub, sub), sub)
            dot = functools.partial(lax.dot_general, dimension_numbers=(((1,), (1,)), ((), ())), preferred_element_type=F32)
            return dot(mine[:, :n], ht[m, cols, :n]) + dot(mine[:, n:], ht[m, cols, :n]) + dot(mine[:, :n], ht[m, cols, n:])

        def finish(t, value):
            load(t).wait()
            block[lax.rem(t, RING)] = block[lax.rem(t, RING)] - value
            store(t).start()

        def work(t, size):
            for k in range(size):
                prefetch(t + k + AHEAD, total)
            values = [product(t + k) for k in range(size)]
            for k in range(size):
                finish(t + k, values[k])

        for k, (start, end) in enumerate(zip([0] + ends, ends)):
            every([rows[j] for j, t in enumerate(stored) if start <= t < end], "wait")
            if k == len(ends) - 1:
                every(hts, "wait")
            if k:
                for u in range(len(floats)):
                    if start <= floats[u] < end:
                        split_tile(u)
            whole = counts[k] + (counts[k + 1] - counts[k]) // GROUP * GROUP

            @pl.loop(counts[k], whole, step=GROUP)
            def _(t):
                work(t, GROUP)

            @pl.loop(whole, counts[k + 1])
            def _(t):
                work(t, 1)

        @pl.loop(jnp.maximum(total - RING, 0), total)
        def _(t):
            store(t).wait()

        every(gone, "wait")
        if keeps_rows:
            for u in range(len(floats)):
                keep_copy(u).wait()


def update(info, pattern, pieces, parts, tiles, ends, near, needed, again, tile, part, cat, schur, rows, keeps_rows, gives):
    n = cat.shape[1]
    width = next(p[3][0].shape[0] for p in pieces if p[3])
    local_rows, local_cols = schur.shape
    sub = min(width, BLOCK)
    count, steps = len(pieces), len(tiles)
    layout = dict(
        pieces=[
            dict(number=a, mask=b, where=w, sources=len(x), ready=None if y is None else y[1], fresh=b is not None)
            for a, b, w, x, y in pieces
        ],
        parts=[(mask, off, size, frm) for mask, off, size, _, frm in parts],
        tiles=tiles,
        ends=ends,
        near=near,
        needed=needed,
        again=again,
        tile=tile,
        sub=sub,
        part=part,
        keeps_rows=keeps_rows,
        gives=gives,
        rows_in=0 if rows is None else 1,
        rows_any=1 if keeps_rows or rows is not None else 0,
    )
    operands = [x for p in pieces for x in p[3]] + [p[4][0] for p in pieces if p[4] is not None] + [p[3] for p in parts] + [cat, schur]
    aliases = {2 + len(operands) - 1: 0}
    shapes = [jax.ShapeDtypeStruct(schur.shape, F32)]
    if rows is not None:
        operands.append(rows)
        aliases[2 + len(operands) - 1] = 1
    if layout["rows_any"]:
        shapes.append(jax.ShapeDtypeStruct((local_rows, 2 * n), BF16))
    if gives:
        shapes.append(jax.ShapeDtypeStruct((count * width, 2 * n), BF16))
    dma = pltpu.SemaphoreType.DMA
    return pl.pallas_call(
        functools.partial(update_kernel, layout),
        out_shape=tuple(shapes),
        grid_spec=pltpu.PrefetchScalarGridSpec(
            num_scalar_prefetch=2,
            grid=(1,),
            in_specs=[ANY] * len(operands),
            out_specs=(ANY,) * len(shapes),
            scratch_shapes=[
                pltpu.VMEM((2 * n, n), BF16),
                pltpu.VMEM((sum(p["fresh"] for p in layout["pieces"]), width, n), F32),
                pltpu.VMEM((count, width, 2 * n), BF16),
                pltpu.VMEM((SLOTS, tile, n), F32),
                pltpu.VMEM((steps * tile, 2 * n), BF16),
                pltpu.VMEM((RING, tile, sub), F32),
                pltpu.SMEM((steps * count * (width // sub) + 1,), jnp.int32),
                dma((2 + count,)),
                dma((count, 2 + len(parts))),
                dma((count,)),
                dma((SLOTS,)),
                dma((steps,)),
                dma((RING,)),
                dma((RING,)),
            ],
        ),
        input_output_aliases=aliases,
        compiler_params=BIG,
        cost_estimate=cost(1000, 1000),
        name="update",
    )(info, pattern, *operands)


def plan(nrow, ncol):
    half, ratio = nrow // 2, ncol // nrow
    if (nrow, ncol) != (4, 8):
        shift = {nrow - 1: 0, nrow - 2: half}
        free = [g for g in range(1, nrow) if g != half]
        for i in range(nrow - 2):
            shift[i] = free[i]
        rounds = [{} for _ in range(nrow)]
        for m in range(nrow):
            for i in range(nrow):
                for j in range(i * ratio):
                    q = m ^ shift[i]
                    rounds[m][i, j] = (divmod(j * nrow + q, ncol), "own", q)
        return rounds
    rounds = [{} for _ in range(4)]

    def at(z, y, x, k):
        return z, (y * 2 + x) * 2 + k

    def put(m, to, frm, kind, x, k):
        rounds[m][at(*to)] = (at(*frm), kind, 2 * x + k)

    first = {0: (0, 1), 1: (0, 0), 2: (1, 0)}
    for z in (1, 2, 3):
        for src in range(z):
            y, x = divmod(src, 2)
            for core in (0, 1):
                half_x = first[src][core] if z != 2 else 1 - first[src][core]
                for m in (0, 1):
                    k = m if z != 1 else 1 - m
                    put(m, (z, y, x, core), (src, core, half_x, k), "own", half_x, k)
    put(2, (3, 0, 0, 0), (0, 0, 0, 0), "x", 1, 0)
    put(2, (3, 0, 0, 1), (0, 0, 0, 1), "y", 0, 1)
    put(3, (3, 0, 0, 0), (0, 0, 0, 1), "x", 1, 1)
    put(3, (3, 0, 0, 1), (0, 1, 1, 0), "x", 0, 0)
    put(2, (3, 0, 1, 0), (1, 0, 1, 0), "own", 1, 0)
    put(2, (3, 0, 1, 1), (1, 0, 1, 1), "y", 1, 1)
    put(3, (3, 0, 1, 0), (1, 0, 1, 1), "own", 1, 1)
    put(3, (3, 0, 1, 1), (1, 1, 1, 0), "own", 1, 0)
    put(2, (3, 1, 0, 1), (2, 1, 0, 0), "x", 1, 0)
    put(2, (3, 1, 0, 0), (2, 1, 0, 1), "y", 0, 1)
    put(3, (3, 1, 0, 1), (2, 1, 1, 1), "own", 1, 1)
    put(3, (3, 1, 0, 0), (2, 1, 0, 0), "y", 0, 0)
    put(2, (2, 0, 0, 0), (3, 0, 0, 0), "a", 0, 0)
    put(3, (2, 0, 0, 0), (3, 0, 0, 0), "b", 0, 1)
    put(2, (2, 0, 0, 1), (3, 0, 0, 1), "a", 1, 0)
    put(3, (2, 0, 0, 1), (0, 1, 1, 1), "own", 1, 1)
    put(2, (2, 0, 1, 0), (3, 0, 1, 0), "a", 0, 0)
    put(3, (2, 0, 1, 0), (3, 0, 1, 0), "b", 0, 1)
    put(2, (2, 0, 1, 1), (3, 0, 1, 1), "a", 0, 0)
    put(3, (2, 0, 1, 1), (1, 1, 0, 1), "own", 0, 1)
    for m in (2, 3):
        put(m, (1, 0, 0, 0), (0, 0, 1, m - 2), "own", 1, m - 2)
        put(m, (1, 0, 0, 1), (0, 1, 0, m - 2), "own", 0, m - 2)
    return rounds


KINDS = ("own", "x", "y", "a", "b")


def tables(nrow, ncol, rounds):
    ratio = ncol // nrow
    tight, half = (nrow, ncol) == (4, 8), nrow // 2
    out = []
    for i in range(nrow):
        for j in range(ncol):
            qs = []
            for m in range(nrow):
                if (i, j) in rounds[m]:
                    qs.append(rounds[m][i, j][2])
                elif tight:
                    qs.append(m ^ (2 * ((j >> 1) & 1)))
                else:
                    qs.append(m)
            masks = [((j * nrow + q) % ncol) ^ j for q in qs]
            sent = [-1] * nrow
            for m in range(nrow):
                for (frm, kind, _) in rounds[m].values():
                    if frm == (i, j):
                        sent[m] = KINDS.index(kind)
            late = int(tight and is_late((i, j)))
            again = int(i == j // ratio and masks[half] > 5)
            out.append([i, j, int(i >= j // ratio), int(i == j // ratio), *qs, *masks, *sent, late, int(i > j // ratio or (i == j // ratio and not again)), again])
    return np.array(out, np.int32)


def is_late(to):
    return to in ((3, 0), (3, 2), (3, 4))


def local(nrow, ncol, front_diag, panel_rows, trailing, pattern):
    local_rows = trailing.shape[0]
    part = panel_rows.shape[0]
    half = nrow // 2
    everyone = [(i, j) for i in range(nrow) for j in range(ncol)]
    rounds = plan(nrow, ncol)
    info = jnp.asarray(tables(nrow, ncol, rounds))[lax.axis_index("row") * ncol + lax.axis_index("col")]
    piece_at, mask_at, sent_at, late_at = 4, 4 + nrow, 4 + 2 * nrow, 4 + 3 * nrow
    barrier = lax.optimization_barrier

    def across(x, mask):
        return lax.ppermute(x, AXES, [(i * ncol + j, i * ncol + (j ^ mask)) for i, j in everyone])

    def send(x, moves):
        return lax.ppermute(x, AXES, [(a * ncol + b, i * ncol + j) for (i, j), ((a, b), _, _) in moves.items()])

    tight = (nrow, ncol) == (4, 8)
    tile = min(BLOCK, part // 2 if tight else part)
    per = part // tile
    below_at = late_at + 1

    def fresh(m, *sources, ready=None):
        return piece_at + m, mask_at + m, late_at, sources, ready

    def cut(parts):
        return [(k, frm + s) for k, (_, _, size, _, frm) in enumerate(parts) for s in range(0, size, tile)]

    def stored(steps):
        return [(None, t * tile) for t in range(steps)]

    def change(pieces, parts, tiles, s, rows, near=0, needed=2, keeps=False, gives=False, ends=None):
        return update(info, pattern, pieces, parts, tiles, ends or [len(tiles)], near, needed, below_at + 1, tile, part, cat, s, rows, keeps, gives)

    near = [m for m in range(2, ncol, 2) if not (tight and m == 6)]
    got = {m: across(panel_rows, m) for m in near}
    col = [send(panel_rows, rounds[m]) for m in range(half)]
    other = across(panel_rows, 1)
    front_diag, info = barrier((front_diag, info))
    diag_factor, inv, schur = factor(front_diag, trailing)
    panel_factor, cat = inverse(inv, panel_rows)
    held, cat = barrier(([panel_rows, other, *[got[m] for m in near], *col], cat))
    own, other, got, col = held[0], held[1], dict(zip(near, held[2:])), held[2 + len(near) :]

    if not tight:
        parts = [(0, 0, part, own, 0), (1, 0, part, other, 0)]
        for m in near:
            parts += [(m, 0, part, got[m], 0), (m + 1, 0, part, across(got[m], 1), 0)]
        col = [*col, *[send(own, rounds[m]) for m in range(half, nrow)]]
        parts.sort(key=lambda p: p[0])
        one, two = [[fresh(m, col[m]) for m in ms] for ms in (range(half), range(half, nrow))]
        schur, rows = change(one, parts, cut(parts), schur, None, keeps=True)
        schur, _ = change(two, parts, stored(ncol * per), schur, rows)
        return (diag_factor, panel_factor, schur)

    h = part // 2
    arrays = [own, got[2], got[4], col[0], col[1]]
    choices = [(k, 0) for k in range(5)]
    segments = [[(0, part, choices, sent_at + m)] for m in (2, 3)] + [[(0, h, [(1, 0)], None)], [(0, h, [(2, h)], None)]]
    c_op, d_op, h1, h2 = pick(info, arrays, segments)
    d_early = send(d_op, {to: move for to, move in rounds[3].items() if not is_late(to)})
    c = send(c_op, rounds[2])
    got[3], got[5] = across(got[2], 1), across(got[4], 1)
    h1, h2 = across(h1, 4), across(h2, 2)
    parts = [(0, 0, part, own, 0), (1, 0, part, other, 0), (2, 0, part, got[2], 0)]
    parts += [(3, 0, part, got[3], 0), (4, 0, part, got[4], 0), (5, 0, part, got[5], 0)]
    schur, rows, ab = change([fresh(0, col[0]), fresh(1, col[1])], parts, cut(parts), schur, None, keeps=True, gives=True)
    d_op, schur = barrier((d_op, schur))
    d_late = send(d_op, {to: move for to, move in rounds[3].items() if is_late(to)})
    beside = [p for p in parts if p[0] in (2, 3)]
    schur, rows, cc = change([fresh(2, c)], beside, stored(6 * per), schur, rows, needed=below_at, gives=True, ends=[3 * per, 6 * per])
    h1, h2, schur = barrier((h1, h2, schur))
    f1, f2 = across(h1, 1), across(h2, 1)
    far = [(6, 0, h, h1, 0), (6, h, h, h2, 0), (7, 0, h, f1, 0), (7, h, h, f2, 0)]
    pieces = [(piece_at + m, None, None, (), (ab, m)) for m in (0, 1)]
    pieces += [fresh(2, ready=(cc, 0)), fresh(3, d_early, d_late)]
    schur, _ = change(pieces, far + beside, stored(6 * per) + cut(far), schur, rows, near=6 * per, ends=[3 * per, 6 * per, 8 * per])
    return (diag_factor, panel_factor, schur)


def solution(mesh):
    nrow, ncol = mesh.shape["row"], mesh.shape["col"]
    return jax.shard_map(
        functools.partial(local, nrow, ncol),
        mesh=mesh,
        in_specs=(P(), P(("row", "col"), None), P("row", "col"), P("row", "col")),
        out_specs=(P(), P(("row", "col"), None), P("row", "col")),
        check_vma=False,
    )
```
